32 devices in a mesh: ep: 16 (over z, x, core), dp: 2 (over y).
Axes of the slice: x: 2, y: 2, z: 4, core: 2. Of those that a mesh axis runs over, the one named last changes fastest.
Arguments:
- tokens: bfloat16 [4096, 2048], P(('dp', 'ep')), parts along dimension 0, may hold values from -6 to 6
- expert_ids: int32 [4096, 8], P(('dp', 'ep')), parts along dimension 0, may hold values from 0 to 15, all different within a row; in each aligned block of 128 rows (0 to 127, 128 to 255, ...) at most 72 rows name the same one
- gate_scores: float32 [4096, 8], P(('dp', 'ep')), parts along dimension 0, may hold values from 0.05 to 1
- gate_weight: bfloat16 [32, 2048, 768], P(('dp', 'ep')), parts along dimension 0, may hold values from -0.125 to 0.125
- up_weight: bfloat16 [32, 2048, 768], P(('dp', 'ep')), parts along dimension 0, may hold values from -0.125 to 0.125
- down_weight: bfloat16 [32, 768, 2048], P(('dp', 'ep')), parts along dimension 0, may hold values from -0.21875 to 0.21875
- partner: int32 [16], replicated, may hold values from 0 to 15, as said below
Outputs:
- mixed: bfloat16 [4096, 2048], P(('dp', 'ep')), parts along dimension 0
The draws below stay inside these ranges and needn't reach their ends.
There are 2 independent parts, one for each index of `dp`. The reference program is written for one: setup_inputs(seed, part) draws one part's arguments, and reference() takes and returns one part's arrays. A program takes and returns all parts, laid end to end along the dimension named above; an argument that names none is the same for every part. Nothing has to cross between parts.
Inputs may be any that keep to these rules, and one draw needn't show every extreme that they name: `expert_ids`: each row names 8 different experts; among the 128 rows of one device no expert is named more than 72 times, a bound that some block reaches. A perfect matching: partner[partner[e]] = e and partner[e] != e for every expert e.
All inputs are finite; a program needn't handle non-finite values.
Results may differ from the reference program's by a relative error of at most 0.0059.
Values may be sent and summed in bfloat16 or wider, within the bound.
No kernel may reach another device: no remote copies, remote signals or barrier semaphores. Data moves between devices by JAX's collectives and lax.ppermute only.
A program may use at most 128 MiB of HBM per device.

```python
import math
import jax
import jax.numpy as jnp
import numpy as np
from jax import lax

D = 2048
FF = 768
TOP = 8
TOK_DEV = 128
EXPERTS = 16
CAP = 72
TOKENS = 2048
N_EP = 16


def draw_partner(key, part):
    key = jax.random.fold_in(key, 11)
    shuffled = jax.random.permutation(key, EXPERTS).astype(jnp.int32)
    swapped = shuffled.reshape(-1, 2)[:, ::-1].reshape(-1)
    return jnp.zeros((EXPERTS,), jnp.int32).at[shuffled].set(swapped)


def levels(stream_key, extent, pieces, smallest, largest):
    loudness, own = 1.0, jax.random.fold_in(stream_key, 6)
    for dim, parts in pieces:
        draws = jnp.exp(jax.random.uniform(jax.random.fold_in(own, dim), (parts,), jnp.float32, smallest / len(pieces), largest / len(pieces)))
        loudness = loudness * jnp.repeat(draws, extent[dim] // parts).reshape([-1 if axis == dim else 1 for axis in range(len(extent))])
    return loudness


def shared_out(own_key, own, number, rows, count, top, reach, skew):
    sequence = jax.random.permutation(own_key, count)
    crowded, common = portions_of(count, rows * top, reach, skew, True), portions_of(count, rows * top, reach, skew, False)
    places = jnp.arange(count)

    def named(sizes, rotation):
        used = int((sizes > 0).sum())
        fixed = max(1, used // 4)
        shifted = fixed + (places - fixed + rotation * (used - fixed)) % max(1, count - fixed)
        return jnp.zeros((count,), jnp.int32).at[sequence[jnp.where(places < fixed, places, shifted)]].set(jnp.asarray(sizes, jnp.int32))

    sizes = jnp.where(number % 4 == 0, named(crowded, number // 4), named(common, number - number // 4 - 1))
    mixed = jax.random.permutation(jax.random.fold_in(own, 3), count)
    giver, taker = mixed[0:count // 2 * 2:2], mixed[1:count // 2 * 2:2]
    room = jnp.minimum(sizes[giver] - 1, reach - sizes[taker]) // 2
    room = jnp.where((giver == sequence[0]) | (taker == sequence[0]) | (sizes[taker] == 0), 0, jnp.maximum(room, 0))
    shifted = jax.random.randint(jax.random.fold_in(own, 4), (count // 2,), 0, 1 << 20) % (room + 1)
    sizes = sizes.at[giver].add(-shifted).at[taker].add(shifted)
    members = jnp.searchsorted(jnp.cumsum(sizes), jnp.arange(rows * top), side="right").astype(jnp.int32)
    table = members.reshape(top, rows).T
    table = table[jax.random.permutation(jax.random.fold_in(own, 1), rows)]
    rotation = jax.random.randint(jax.random.fold_in(own, 2), (rows, 1), 0, top)
    return jnp.take_along_axis(table, (jnp.arange(top)[None, :] + rotation) % top, axis=1)


def portions_of(count, total, reach, slope, full):
    weights = [(1 << 20) // math.isqrt(grade ** slope) + 1 for grade in range(1, count + 1)]
    largest = reach if full else min(reach, max(-(-total // count), total * weights[0] // sum(weights)))
    least = 1 if total - largest >= count - 1 else 0
    counts, spare = [largest] + [least] * (count - 1), total - largest - least * (count - 1)
    while spare > 0:
        candidates = [i for i in range(1, count) if counts[i] < largest] or [i for i in range(1, count) if counts[i] < reach]
        whole, left = sum([weights[i] for i in candidates]), spare
        for i in candidates:
            extra = min(reach - counts[i], max(1, left * weights[i] // whole), spare)
            counts[i] = counts[i] + extra
            spare = spare - extra
    return np.array(counts)


def normal_values(key, shape, scale, limit, cuts=(), kind=jnp.bfloat16):
    result = scale * jax.random.normal(key, shape, jnp.float32)
    if cuts:
        result = result * levels(key, shape, cuts, -0.22, 0.18)
    return jnp.clip(result, -limit, limit).astype(kind)


def setup_inputs(seed: int = 0, part: int = 0) -> dict:
    seeds = jax.random.split(jax.random.key(seed), 8)
    part_splits = jax.random.split(jax.random.fold_in(seeds[7], part), 8)
    tokens = normal_values(part_splits[0], (TOKENS, D), 1.0, 6.0, ((0, 16),))
    expert_ids_keys = jax.random.split(jax.random.fold_in(part_splits[1], 1), TOKENS // TOK_DEV)
    expert_ids_turns = jax.random.permutation(jax.random.fold_in(part_splits[1], 3), TOKENS // TOK_DEV)
    expert_ids = jax.vmap(lambda own, number: shared_out(jax.random.fold_in(part_splits[1], 2), own, number, TOK_DEV, EXPERTS, TOP, CAP, 2))(expert_ids_keys, expert_ids_turns).reshape((TOKENS, TOP))
    gate_scores = jnp.clip(jnp.exp(math.log(1.0) - 2.9957323 * jax.random.uniform(part_splits[2], (TOKENS, TOP), jnp.float32) ** levels(part_splits[2], (TOKENS, TOP), ((0, 16),), -0.2, 0.2)), 0.05, 1.0)
    gate_weight = normal_values(part_splits[3], (EXPERTS, D, FF), D ** -0.5, 0.125, ((0, 16),))
    up_weight = normal_values(part_splits[4], (EXPERTS, D, FF), D ** -0.5, 0.125, ((0, 16),))
    down_weight = normal_values(part_splits[5], (EXPERTS, FF, D), FF ** -0.5, 0.21875, ((0, 16),))
    partner = draw_partner(jax.random.fold_in(seeds[7], 71), part)
    return dict(tokens=tokens, expert_ids=expert_ids, gate_scores=gate_scores, gate_weight=gate_weight, up_weight=up_weight, down_weight=down_weight, partner=partner)


def expert_rows(inputs, w_gate, w_up, w_down):
    gate_proj = jnp.dot(inputs, w_gate, preferred_element_type=jnp.float32)
    up_proj = jnp.dot(inputs, w_up, preferred_element_type=jnp.float32)
    hidden = (jax.nn.silu(gate_proj) * up_proj).astype(jnp.bfloat16)
    return jnp.dot(hidden, w_down, preferred_element_type=jnp.float32).astype(jnp.bfloat16)


def reference(tokens, expert_ids, gate_scores, gate_weight, up_weight, down_weight, partner):
    flat_ids = expert_ids.reshape(-1)
    flat_scores = gate_scores.reshape(-1)
    live_limit = N_EP * CAP

    def add_expert(accumulated, expert):
        chosen = flat_ids == expert
        positions = jnp.nonzero(chosen, size=live_limit, fill_value=0)[0].astype(jnp.int32)
        is_live = jnp.arange(live_limit, dtype=jnp.int32) < jnp.sum(chosen.astype(jnp.int32))
        token_index = positions // TOP
        source_slot = partner[expert]
        result_rows = expert_rows(tokens[token_index], gate_weight[source_slot], up_weight[source_slot], down_weight[source_slot])
        scaling = jnp.where(is_live, flat_scores[positions], jnp.zeros_like(flat_scores[positions]))
        accumulated = accumulated.at[token_index].add(result_rows.astype(jnp.float32) * scaling[:, None])
        return accumulated, None

    start = jnp.zeros((TOKENS, D), jnp.float32)
    accumulated, _ = lax.scan(add_expert, start, jnp.arange(EXPERTS, dtype=jnp.int32))
    return accumulated.astype(jnp.bfloat16)
```

```python
import functools

import jax
import jax.numpy as jnp
from jax import lax
from jax.experimental import pallas as pl
from jax.experimental.pallas import tpu as pltpu
from jax.sharding import PartitionSpec as P


def ffn_kernel(n_in, tiles, *refs):
    x_refs, refs = refs[:n_in], refs[n_in:]
    w_ref, weights, refs = refs[0], refs[1:7], refs[7:]
    out_refs, (rows, total) = refs[:n_in], refs[n_in:]
    step = pl.program_id(0)
    half = x_refs[0].shape[0]

    @pl.when(step == 0)
    def _():
        for i, x_ref in enumerate(x_refs):
            rows[pl.ds(i * half, half), :] = x_ref[...]
        total[...] = jnp.zeros_like(total)

    def add_tile(expert, gate_ref, up_ref, down_ref):
        x = rows[...]
        gate = jnp.dot(x, gate_ref[0], preferred_element_type=jnp.float32)
        up = jnp.dot(x, up_ref[0], preferred_element_type=jnp.float32)
        hidden = (gate / (1.0 + jnp.exp(-gate)) * up).astype(jnp.bfloat16)
        out = jnp.dot(hidden, down_ref[0], preferred_element_type=jnp.float32)
        total[...] += out * w_ref[:, expert : expert + 1]

    @pl.when(step < tiles)
    def _():
        add_tile(0, *weights[:3])

    @pl.when(step >= tiles)
    def _():
        add_tile(1, *weights[3:])

    @pl.when(step == 2 * tiles - 1)
    def _():
        for i, out_ref in enumerate(out_refs):
            out_ref[...] = total[pl.ds(i * half, half), :].astype(out_ref.dtype)


def ffn(blocks, kinds, scores, own, other):
    half, width = blocks[0].shape
    ff = own[0].shape[2]
    tile = 256
    tiles = ff // tile
    n_in = len(blocks)
    m = n_in * half
    whole = pl.BlockSpec((half, width), lambda i: (0, 0))

    def spec(first):
        at = (lambda i: jnp.minimum(i, tiles - 1)) if first else (lambda i: jnp.maximum(i - tiles, 0))
        return [
            pl.BlockSpec((1, width, tile), lambda i: (0, 0, at(i))),
            pl.BlockSpec((1, width, tile), lambda i: (0, 0, at(i))),
            pl.BlockSpec((1, tile, width), lambda i: (0, at(i), 0)),
        ]

    return pl.pallas_call(
        functools.partial(ffn_kernel, n_in, tiles),
        grid=(2 * tiles,),
        in_specs=[whole] * n_in + [pl.BlockSpec((m, 2), lambda i: (0, 0))] + spec(True) + spec(False),
        out_specs=[whole] * n_in,
        out_shape=[jax.ShapeDtypeStruct((half, width), kind) for kind in kinds],
        scratch_shapes=[pltpu.VMEM((m, width), jnp.bfloat16), pltpu.VMEM((m, width), jnp.float32)],
        compiler_params=pltpu.CompilerParams(vmem_limit_bytes=40 * 2**20),
        cost_estimate=pl.CostEstimate(
            flops=12 * m * width * ff, bytes_accessed=12 * width * ff + 6 * m * width, transcendentals=2 * m * ff
        ),
    )(*blocks, scores, *own, *other)


def ring_order(chips):
    return list(range(0, chips, 2)) + list(range(1, chips, 2))[::-1]


def on_device(tokens, expert_ids, gate_scores, gate_weight, up_weight, down_weight, partner):
    n_dev = lax.axis_size("ep")
    chips = n_dev // 2
    far = chips // 2
    rows, width = tokens.shape
    half = rows // 2
    order = ring_order(chips)
    forward = [(order[i] * 2 + k, order[(i + 1) % chips] * 2 + k) for i in range(chips) for k in range(2)]
    backward = [(b, a) for a, b in forward]
    swap = [(i, i ^ 1) for i in range(n_dev)]
    perm = (forward, backward)

    other = tuple(lax.ppermute(w, "ep", swap) for w in (gate_weight, up_weight, down_weight))
    own = (gate_weight, up_weight, down_weight)

    slot_scores = jnp.sum(
        jnp.where(expert_ids.T[None] == partner[:, None, None], gate_scores.T[None], 0.0), axis=1
    )
    all_scores = lax.all_gather(slot_scores, "ep", axis=0).reshape(chips, 2, n_dev, rows)
    me = lax.axis_index("ep")
    core = me % 2
    chip = me // 2
    mine = lax.dynamic_index_in_dim(all_scores, core, 1, keepdims=False)
    mine = jnp.stack(
        [
            lax.dynamic_index_in_dim(mine, me, 1, keepdims=False),
            lax.dynamic_index_in_dim(mine, chip * 2 + 1 - core, 1, keepdims=False),
        ],
        axis=-1,
    )
    place = jnp.where(chip % 2 == 0, chip // 2, chips - 1 - chip // 2)
    mine = mine[jnp.asarray(order, jnp.int32)]
    mine = jnp.concatenate([mine, mine], axis=0)

    def scores_of(distance, h):
        block = lax.dynamic_index_in_dim(mine, (place + distance) % chips, 0, keepdims=False)
        return block[h * half : (h + 1) * half]

    halves = (tokens[:half], tokens[half:])
    held = [[[halves[h]] for h in range(2)] for _ in range(2)]
    last = [[far if d == h else far - 1 for h in range(2)] for d in range(2)]
    for s in range(1, far + 1):
        for h in range(2):
            for d in range(2):
                if s <= last[d][h]:
                    held[d][h].append(lax.ppermute(held[d][h][-1], "ep", perm[d]))

    done = {}

    def compute(keys):
        blocks = [held[d][h][s] for d, h, s in keys]
        kinds = [jnp.bfloat16 if s == last[d][h] else jnp.float32 for d, h, s in keys]
        scores = jnp.concatenate([scores_of(-s if d == 0 else s, h) for d, h, s in keys], axis=0)
        for key, out in zip(keys, ffn(blocks, kinds, scores, own, other)):
            done[key] = out

    compute([(0, 0, 0), (0, 1, 0)] + [(d, h, 1) for d in range(2) for h in range(2)])
    for s in range(2, far + 1):
        compute([(d, h, s) for d in range(2) for h in range(2) if s <= last[d][h]])

    back = {}
    for s in range(far, 0, -1):
        for h in range(2):
            for d in range(2):
                if s > last[d][h]:
                    continue
                part = done[d, h, s]
                if (d, h) in back:
                    part = (back[d, h].astype(jnp.float32) + part).astype(jnp.bfloat16)
                back[d, h] = lax.ppermute(part, "ep", perm[1 - d])
    out = [
        (done[0, h, 0] + back[0, h].astype(jnp.float32) + back[1, h].astype(jnp.float32)).astype(jnp.bfloat16)
        for h in range(2)
    ]
    return jnp.concatenate(out, axis=0)


def solution(mesh):
    rows = P(("dp", "ep"), None)
    stacks = P(("dp", "ep"), None, None)
    return jax.shard_map(
        on_device,
        mesh=mesh,
        in_specs=(rows, rows, rows, stacks, stacks, stacks, P()),
        out_specs=rows,
        check_vma=False,
    )
```

```python
import functools

import jax
import jax.numpy as jnp
from jax import lax
from jax.experimental import pallas as pl
from jax.experimental.pallas import tpu as pltpu
from jax.sharding import PartitionSpec as P

LANES = 128


def pack_kernel(n_dev, tokens_ref, ids_ref, scores_ref, partner_ref, out_ref):
    rows, width = tokens_ref.shape
    extra = out_ref.shape[1] - width
    lane = lax.broadcasted_iota(jnp.int32, (extra, 1), 0)
    served = jnp.full((extra, 1), -1, jnp.int32)
    for slot in range(n_dev):
        hit = (lane == slot) | (lane == slot + n_dev)
        served = jnp.where(hit, partner_ref[slot], served)
    total = jnp.zeros((extra, rows), jnp.float32)
    for k in range(ids_ref.shape[0]):
        total += jnp.where(ids_ref[k : k + 1, :] == served, scores_ref[k : k + 1, :], 0.0)
    high = total.astype(jnp.bfloat16).astype(jnp.float32)
    tail = jnp.where(lane < n_dev, high, total - high).T.astype(jnp.bfloat16)
    out_ref[:, :width] = tokens_ref[...]
    out_ref[:, width:] = tail


def pack(tokens, expert_ids, gate_scores, partner, n_dev):
    rows, width = tokens.shape
    extra = -(-2 * n_dev // LANES) * LANES
    near = pl.BlockSpec(memory_space=pltpu.VMEM)
    return pl.pallas_call(
        functools.partial(pack_kernel, n_dev),
        in_specs=[near, near, near, pl.BlockSpec(memory_space=pltpu.SMEM)],
        out_specs=near,
        out_shape=jax.ShapeDtypeStruct((rows, width + extra), jnp.bfloat16),
        compiler_params=pltpu.CompilerParams(vmem_limit_bytes=6 * 2**20),
    )(tokens, expert_ids.T, gate_scores.T, partner)


def ffn_kernel(n_in, n_out, n_dev, *refs):
    x_refs, weights, refs = refs[:n_in], refs[n_in : n_in + 6], refs[n_in + 6 :]
    out_refs, (rows, total) = refs[:n_out], refs[n_out:]
    half = out_refs[0].shape[0]
    width = total.shape[1]
    me = lax.axis_index("ep")
    slots = (me, me + 1 - 2 * (me % 2))
    tails = []
    at = 0
    for x_ref in x_refs:
        rows[pl.ds(at, x_ref.shape[0]), :] = x_ref[:, :width]
        tails.append(x_ref[:, width:].astype(jnp.float32))
        at += x_ref.shape[0]
    tails = jnp.concatenate(tails, axis=0)
    lane = lax.broadcasted_iota(jnp.int32, tails.shape, 1)
    for expert, slot in enumerate(slots):
        hit = (lane == slot) | (lane == slot + n_dev)
        score = jnp.sum(jnp.where(hit, tails, 0.0), axis=1, keepdims=True)
        gate_ref, up_ref, down_ref = weights[3 * expert : 3 * expert + 3]
        x = rows[...]
        gate = jnp.dot(x, gate_ref[0], preferred_element_type=jnp.float32)
        up = jnp.dot(x, up_ref[0], preferred_element_type=jnp.float32)
        hidden = (gate / (1.0 + jnp.exp(-gate)) * up).astype(jnp.bfloat16)
        out = jnp.dot(hidden, down_ref[0], preferred_element_type=jnp.float32) * score
        if expert == 0:
            total[...] = out
        else:
            out = total[...] + out
            for i, out_ref in enumerate(out_refs):
                out_ref[...] = out[i * half : (i + 1) * half].astype(out_ref.dtype)


def ffn(blocks, half, kinds, own, other, n_dev):
    _, width, ff = own[0].shape
    m = sum(block.shape[0] for block in blocks)
    n_in, n_out = len(blocks), len(kinds)
    near = pl.BlockSpec(memory_space=pltpu.VMEM)
    return pl.pallas_call(
        functools.partial(ffn_kernel, n_in, n_out, n_dev),
        in_specs=[near] * (n_in + 6),
        out_specs=[near] * n_out,
        out_shape=[jax.ShapeDtypeStruct((half, width), kind) for kind in kinds],
        scratch_shapes=[pltpu.VMEM((m, width), jnp.bfloat16), pltpu.VMEM((m, width), jnp.float32)],
        compiler_params=pltpu.CompilerParams(vmem_limit_bytes=16 * 2**20),
        cost_estimate=pl.CostEstimate(
            flops=12 * m * width * ff, bytes_accessed=12 * width * ff + 6 * m * width, transcendentals=2 * m * ff
        ),
    )(*blocks, *own, *other)


def ring_order(chips):
    return list(range(0, chips, 2)) + list(range(1, chips, 2))[::-1]


def on_device(tokens, expert_ids, gate_scores, gate_weight, up_weight, down_weight, partner):
    n_dev = lax.axis_size("ep")
    chips = n_dev // 2
    far = chips // 2
    order = ring_order(chips)

    def shift(by):
        return [(order[i] * 2 + k, order[(i + by) % chips] * 2 + k) for i in range(chips) for k in range(2)]

    perm = (shift(1), shift(-1))
    swap = [(i, i ^ 1) for i in range(n_dev)]
    own = (gate_weight, up_weight, down_weight)

    def tie(value, *deps):
        return lax.optimization_barrier((value, deps))[0]

    packed = pack(tokens, expert_ids, gate_scores, partner, n_dev)
    half = tokens.shape[0] // 2
    other = [lax.ppermute(w, "ep", swap) for w in own]
    first = [lax.ppermute(packed, "ep", perm[d]) for d in range(2)]
    held = {(d, h, 1): block[h * half : (h + 1) * half] for d, block in enumerate(first) for h in range(2)}
    last = {(d, h): far if d == h else far - 1 for d in range(2) for h in range(2)}

    def keys(s):
        if s == 0:
            return [(0, 0, 0), (0, 1, 0)]
        return [(d, h, s) for h in range(2) for d in range(2) if s <= last[d, h]]

    done = {}

    def compute(s, blocks):
        names = [(d, h, 1) for d in range(2) for h in range(2)] if s == 1 else keys(s)
        kinds = [jnp.bfloat16 if n[2] and n[2] == last[n[:2]] else jnp.float32 for n in names]
        done.update(zip(names, ffn(blocks, half, kinds, own, other, n_dev)))

    for s in range(1, far + 1):
        if s > 1:
            for d, h, _ in keys(s):
                deps = other if s == 2 else [done[keys(s - 2)[0]]]
                if s == 3:
                    deps = deps + [done[keys(0)[0]]]
                if s == far:
                    deps = deps + [held[d, 1 - h, s - 1]]
                held[d, h, s] = lax.ppermute(tie(held[d, h, s - 1], *deps), "ep", perm[d])
        blocks = first if s == 1 else [held[k] for k in keys(s)]
        compute(s, blocks if s == 1 else tie(blocks, done[keys(s - 1)[0]]))
        if s == 1:
            compute(0, [packed])
    for k in keys(far - 1):
        done[k] = tie(done[k], *[held[k] for k in keys(far)])

    back = {}
    for s in range(far, 0, -1):
        for d, h, _ in keys(s):
            part = done[d, h, s]
            if (d, h) in back:
                part = (back[d, h].astype(jnp.float32) + part).astype(jnp.bfloat16)
            back[d, h] = lax.ppermute(part, "ep", perm[1 - d])
    out = [
        (done[0, h, 0] + back[0, h].astype(jnp.float32) + back[1, h].astype(jnp.float32)).astype(jnp.bfloat16)
        for h in range(2)
    ]
    return jnp.concatenate(out, axis=0)


def solution(mesh):
    rows = P(("dp", "ep"), None)
    stacks = P(("dp", "ep"), None, None)
    return jax.shard_map(
        on_device,
        mesh=mesh,
        in_specs=(rows, rows, rows, stacks, stacks, stacks, P()),
        out_specs=rows,
        check_vma=False,
    )
```

```python
import functools

import jax
import jax.numpy as jnp
from jax import lax
from jax.experimental import pallas as pl
from jax.experimental.pallas import tpu as pltpu
from jax.sharding import PartitionSpec as P

LANES = 128


def pack_kernel(tokens_ref, scores_ref, out_ref):
    rows, width = tokens_ref.shape
    n_dev = scores_ref.shape[0]
    scores = scores_ref[...]
    high = scores.astype(jnp.bfloat16).astype(jnp.float32)
    blank = jnp.zeros((out_ref.shape[1] - width - 2 * n_dev, rows), jnp.float32)
    parts = [high, scores - high] + ([blank] if blank.shape[0] else [])
    out_ref[:, :width] = tokens_ref[...]
    out_ref[:, width:] = jnp.concatenate(parts, axis=0).T.astype(jnp.bfloat16)


def pack(tokens, expert_ids, gate_scores, partner, n_dev):
    scores = jnp.sum(jnp.where(expert_ids.T[None] == partner[:, None, None], gate_scores.T[None], 0.0), axis=1)
    rows, width = tokens.shape
    extra = -(-2 * n_dev // LANES) * LANES
    near = pl.BlockSpec(memory_space=pltpu.VMEM)
    return pl.pallas_call(
        pack_kernel,
        in_specs=[near, near],
        out_specs=near,
        out_shape=jax.ShapeDtypeStruct((rows, width + extra), jnp.bfloat16),
        compiler_params=pltpu.CompilerParams(vmem_limit_bytes=4 * 2**20),
    )(tokens, scores)


def load_kernel(*refs):
    n = len(refs) // 2
    sources, targets, sems = refs[:n], refs[n : 2 * n], refs[-1]
    copies = [pltpu.make_async_copy(a, b, sems.at[i]) for i, (a, b) in enumerate(zip(sources, targets))]
    for copy in copies:
        copy.start()
    for copy in copies:
        copy.wait()


def load(arrays):
    return pl.pallas_call(
        load_kernel,
        in_specs=[pl.BlockSpec(memory_space=pltpu.HBM)] * len(arrays),
        out_specs=[pl.BlockSpec(memory_space=pltpu.VMEM)] * len(arrays),
        out_shape=[jax.ShapeDtypeStruct(a.shape, a.dtype) for a in arrays],
        scratch_shapes=[pltpu.SemaphoreType.DMA((len(arrays),))],
        compiler_params=pltpu.CompilerParams(vmem_limit_bytes=16 * 2**20),
        cost_estimate=pl.CostEstimate(
            flops=0, bytes_accessed=sum(a.size * a.dtype.itemsize for a in arrays), transcendentals=0
        ),
    )(*arrays)


def ffn_kernel(n_in, n_out, n_dev, *refs):
    x_refs, weights, refs = refs[:n_in], refs[n_in : n_in + 6], refs[n_in + 6 :]
    out_refs, (rows, total) = refs[:n_out], refs[n_out:]
    half = out_refs[0].shape[0]
    width = total.shape[1]
    me = lax.axis_index("ep")
    slots = (me, me + 1 - 2 * (me % 2))
    tails = []
    at = 0
    for x_ref in x_refs:
        rows[pl.ds(at, x_ref.shape[0]), :] = x_ref[:, :width]
        tails.append(x_ref[:, width:].astype(jnp.float32))
        at += x_ref.shape[0]
    tails = jnp.concatenate(tails, axis=0)
    lane = lax.broadcasted_iota(jnp.int32, tails.shape, 1)
    for expert, slot in enumerate(slots):
        hit = (lane == slot) | (lane == slot + n_dev)
        score = jnp.sum(jnp.where(hit, tails, 0.0), axis=1, keepdims=True)
        gate_ref, up_ref, down_ref = weights[3 * expert : 3 * expert + 3]
        x = rows[...]
        gate = jnp.dot(x, gate_ref[0], preferred_element_type=jnp.float32)
        up = jnp.dot(x, up_ref[0], preferred_element_type=jnp.float32)
        hidden = (gate / (1.0 + jnp.exp(-gate)) * up).astype(jnp.bfloat16)
        out = jnp.dot(hidden, down_ref[0], preferred_element_type=jnp.float32) * score
        if expert == 0:
            total[...] = out
        else:
            out = total[...] + out
            for i, out_ref in enumerate(out_refs):
                out_ref[...] = out[i * half : (i + 1) * half].astype(out_ref.dtype)


def ffn(blocks, half, kinds, own, other, n_dev):
    _, width, ff = own[0].shape
    m = sum(block.shape[0] for block in blocks)
    n_in, n_out = len(blocks), len(kinds)
    near = pl.BlockSpec(memory_space=pltpu.VMEM)
    return pl.pallas_call(
        functools.partial(ffn_kernel, n_in, n_out, n_dev),
        in_specs=[near] * (n_in + 6),
        out_specs=[near] * n_out,
        out_shape=[jax.ShapeDtypeStruct((half, width), kind) for kind in kinds],
        scratch_shapes=[pltpu.VMEM((m, width), jnp.bfloat16), pltpu.VMEM((m, width), jnp.float32)],
        compiler_params=pltpu.CompilerParams(vmem_limit_bytes=16 * 2**20),
        cost_estimate=pl.CostEstimate(
            flops=12 * m * width * ff, bytes_accessed=12 * width * ff + 6 * m * width, transcendentals=2 * m * ff
        ),
    )(*blocks, *own, *other)


def ring_order(chips):
    return list(range(0, chips, 2)) + list(range(1, chips, 2))[::-1]


def on_device(tokens, expert_ids, gate_scores, gate_weight, up_weight, down_weight, partner):
    n_dev = lax.axis_size("ep")
    chips = n_dev // 2
    far = chips // 2
    order = ring_order(chips)

    def shift(by):
        return [(order[i] * 2 + k, order[(i + by) % chips] * 2 + k) for i in range(chips) for k in range(2)]

    perm = (shift(1), shift(-1))
    swap = [(i, i ^ 1) for i in range(n_dev)]
    own = (gate_weight, up_weight, down_weight)

    def tie(value, *deps):
        return lax.optimization_barrier((value, deps))[0]

    half = tokens.shape[0] // 2
    other = [lax.ppermute(w, "ep", swap) for w in own]
    packed = pack(tokens, expert_ids, gate_scores, partner, n_dev)
    first = [lax.ppermute(packed, "ep", perm[d]) for d in range(2)]
    own = load(own)
    held = {(d, h, 1): block[h * half : (h + 1) * half] for d, block in enumerate(first) for h in range(2)}
    last = {(d, h): far if d == h else far - 1 for d in range(2) for h in range(2)}
    done = {}

    def compute(names, blocks, *deps):
        kinds = [jnp.bfloat16 if n[2] and n[2] == last[n[:2]] else jnp.float32 for n in names]
        blocks = tie(blocks, *deps) if deps else blocks
        done.update(zip(names, ffn(blocks, half, kinds, own, other, n_dev)))
        return done[names[0]]

    def send(names, *deps):
        for d, h, s in names:
            held[d, h, s] = lax.ppermute(tie(held[d, h, s - 1], *deps), "ep", perm[d])

    groups = ([(0, 0), (1, 1)], [(1, 0), (0, 1)])

    def flows(g, s):
        return [(d, h, s) for d, h in groups[g] if s <= last[d, h]]

    for g in range(2):
        send(flows(g, 2), *other, *own)
    worked = []
    for s in range(1, far):
        for g in range(2):
            names = flows(g, s)
            worked.append(compute(names, [held[n] for n in names], *worked[-1:]))
            if s + 2 <= far:
                send(flows(g, s + 2), worked[-1])
    names = flows(0, far)
    worked.append(compute(names, [held[n] for n in names], worked[-1]))

    back = {}

    def give(names, *deps):
        for d, h, s in names:
            part = done[d, h, s]
            if (d, h) in back:
                part = (tie(back[d, h], *deps).astype(jnp.float32) + part).astype(jnp.bfloat16)
            back[d, h] = lax.ppermute(part, "ep", perm[1 - d])

    give(flows(1, far - 1))
    give(flows(0, far))
    for s in range(far - 1, 0, -1):
        if s > 1:
            give(flows(1, s - 1), worked[-1])
        give(flows(0, s))
    compute([(0, 0, 0), (0, 1, 0)], [packed], worked[-1])
    out = [
        (done[0, h, 0] + back[0, h].astype(jnp.float32) + back[1, h].astype(jnp.float32)).astype(jnp.bfloat16)
        for h in range(2)
    ]
    return jnp.concatenate(out, axis=0)


def solution(mesh):
    rows = P(("dp", "ep"), None)
    stacks = P(("dp", "ep"), None, None)
    return jax.shard_map(
        on_device,
        mesh=mesh,
        in_specs=(rows, rows, rows, stacks, stacks, stacks, P()),
        out_specs=rows,
        check_vma=False,
    )
```

```python
import functools

import jax
import jax.numpy as jnp
from jax import lax
from jax.experimental import pallas as pl
from jax.experimental.pallas import tpu as pltpu
from jax.sharding import PartitionSpec as P

LANES = 128
TILE = 16


def pack_kernel(tokens_ref, scores_ref, out_ref):
    rows, width = tokens_ref.shape
    chips = scores_ref.shape[0] // 2
    half = rows // 2
    lane = lax.broadcasted_iota(jnp.int32, (chips, LANES), 1)
    even, odd = (scores_ref[pl.ds(i, chips, stride=2), :] for i in range(2))
    at = 0
    for h in range(2):
        for g in range(0, half, TILE):
            for j in range(0, width, LANES):
                out_ref[pl.ds(at, TILE), :] = tokens_ref[pl.ds(h * half + g, TILE), pl.ds(j, LANES)]
                at += TILE
        first, second = (even, pltpu.roll(odd, half, 1)) if h == 0 else (pltpu.roll(even, half, 1), odd)
        scores = jnp.where(lane < half, first, second)
        high = scores.astype(jnp.bfloat16).astype(jnp.float32)
        tail = jnp.concatenate([high, scores - high], axis=0).astype(jnp.bfloat16)
        out_ref[pl.ds(at, 2 * chips), :] = tail
        at += 2 * chips


def pack(tokens, expert_ids, gate_scores, partner):
    scores = jnp.sum(jnp.where(expert_ids.T[None] == partner[:, None, None], gate_scores.T[None], 0.0), axis=1)
    rows, width = tokens.shape
    near = pl.BlockSpec(memory_space=pltpu.VMEM)
    return pl.pallas_call(
        pack_kernel,
        in_specs=[near, near],
        out_specs=near,
        out_shape=jax.ShapeDtypeStruct((rows * width // LANES + 2 * scores.shape[0], LANES), jnp.bfloat16),
        compiler_params=pltpu.CompilerParams(vmem_limit_bytes=4 * 2**20),
    )(tokens, scores)


def load_kernel(*refs):
    n = len(refs) // 2
    sources, targets, sems = refs[:n], refs[n : 2 * n], refs[-1]
    copies = [pltpu.make_async_copy(a, b, sems.at[i]) for i, (a, b) in enumerate(zip(sources, targets))]
    for copy in copies:
        copy.start()
    for copy in copies:
        copy.wait()


def load(arrays):
    return pl.pallas_call(
        load_kernel,
        in_specs=[pl.BlockSpec(memory_space=pltpu.HBM)] * len(arrays),
        out_specs=[pl.BlockSpec(memory_space=pltpu.VMEM)] * len(arrays),
        out_shape=[jax.ShapeDtypeStruct(a.shape, a.dtype) for a in arrays],
        scratch_shapes=[pltpu.SemaphoreType.DMA((len(arrays),))],
        compiler_params=pltpu.CompilerParams(vmem_limit_bytes=16 * 2**20),
        cost_estimate=pl.CostEstimate(
            flops=0, bytes_accessed=sum(a.size * a.dtype.itemsize for a in arrays), transcendentals=0
        ),
    )(*arrays)


def ffn_kernel(n_in, n_out, n_dev, *refs):
    x_refs, weights, refs = refs[:n_in], refs[n_in : n_in + 6], refs[n_in + 6 :]
    out_refs, (rows, total) = refs[:n_out], refs[n_out:]
    half, width = out_refs[0].shape
    me = lax.axis_index("ep")
    chip, core = me // 2, me % 2
    row = lax.broadcasted_iota(jnp.int32, (n_dev, LANES), 0)
    hit = (row == chip) | (row == chip + n_dev // 2)
    columns = []
    for x_ref in x_refs:
        at = 0
        while at < x_ref.shape[0]:
            for g in range(0, half, TILE):
                for j in range(0, width, LANES):
                    rows[pl.ds(len(columns) * half + g, TILE), pl.ds(j, LANES)] = x_ref[pl.ds(at, TILE), :]
                    at += TILE
            tail = jnp.where(hit, x_ref[pl.ds(at, n_dev), :].astype(jnp.float32), 0.0)
            both = jnp.broadcast_to(jnp.sum(tail, axis=0, keepdims=True), (LANES, LANES)).T[:, 0:1]
            columns.append((both[:half], both[half:]))
            at += n_dev
    first, second = (jnp.concatenate([pair[i] for pair in columns], axis=0) for i in range(2))
    for expert in range(2):
        score = jnp.where(core == expert, first, second)
        gate_ref, up_ref, down_ref = weights[3 * expert : 3 * expert + 3]
        x = rows[...]
        gate = jnp.dot(x, gate_ref[0], preferred_element_type=jnp.float32)
        up = jnp.dot(x, up_ref[0], preferred_element_type=jnp.float32)
        hidden = (gate / (1.0 + jnp.exp(-gate)) * up).astype(jnp.bfloat16)
        out = jnp.dot(hidden, down_ref[0], preferred_element_type=jnp.float32) * score
        if expert == 0:
            total[...] = out
        else:
            out = total[...] + out
            for i, out_ref in enumerate(out_refs):
                out_ref[...] = out[i * half : (i + 1) * half].astype(out_ref.dtype)


def ffn(blocks, half, kinds, own, other, n_dev):
    _, width, ff = own[0].shape
    n_in, n_out = len(blocks), len(kinds)
    m = n_out * half
    near = pl.BlockSpec(memory_space=pltpu.VMEM)
    return pl.pallas_call(
        functools.partial(ffn_kernel, n_in, n_out, n_dev),
        in_specs=[near] * (n_in + 6),
        out_specs=[near] * n_out,
        out_shape=[jax.ShapeDtypeStruct((half, width), kind) for kind in kinds],
        scratch_shapes=[pltpu.VMEM((m, width), jnp.bfloat16), pltpu.VMEM((m, width), jnp.float32)],
        compiler_params=pltpu.CompilerParams(vmem_limit_bytes=16 * 2**20),
        cost_estimate=pl.CostEstimate(
            flops=12 * m * width * ff, bytes_accessed=12 * width * ff + 6 * m * width, transcendentals=2 * m * ff
        ),
    )(*blocks, *own, *other)


def ring_order(chips):
    return list(range(0, chips, 2)) + list(range(1, chips, 2))[::-1]


def on_device(tokens, expert_ids, gate_scores, gate_weight, up_weight, down_weight, partner):
    n_dev = lax.axis_size("ep")
    chips = n_dev // 2
    far = chips // 2
    order = ring_order(chips)

    def shift(by):
        return [(order[i] * 2 + k, order[(i + by) % chips] * 2 + k) for i in range(chips) for k in range(2)]

    perm = (shift(1), shift(-1))
    swap = [(i, i ^ 1) for i in range(n_dev)]
    own = (gate_weight, up_weight, down_weight)

    def tie(value, *deps):
        return lax.optimization_barrier((value, deps))[0]

    half = tokens.shape[0] // 2
    other = [lax.ppermute(w, "ep", swap) for w in own]
    packed = pack(tokens, expert_ids, gate_scores, partner)
    first = [lax.ppermute(packed, "ep", perm[d]) for d in range(2)]
    own = load(own)
    held = {(d, h, 1): part for d, block in enumerate(first) for h, part in enumerate(jnp.split(block, 2))}
    last = {(d, h): far if d == h else far - 1 for d in range(2) for h in range(2)}
    done = {}

    def compute(names, blocks, *deps):
        kinds = [jnp.bfloat16 if n[2] and n[2] == last[n[:2]] else jnp.float32 for n in names]
        blocks = tie(blocks, *deps) if deps else blocks
        done.update(zip(names, ffn(blocks, half, kinds, own, other, n_dev)))
        return done[names[0]]

    def send(names, *deps):
        for d, h, s in names:
            held[d, h, s] = lax.ppermute(tie(held[d, h, s - 1], *deps), "ep", perm[d])

    groups = ([(0, 0), (1, 1)], [(1, 0), (0, 1)])

    def flows(g, s):
        return [(d, h, s) for d, h in groups[g] if s <= last[d, h]]

    for g in range(2):
        send(flows(g, 2), *other, *own)
    worked = []
    for s in range(1, far):
        for g in range(2):
            names = flows(g, s)
            worked.append(compute(names, [held[n] for n in names], *worked[-1:]))
            if s + 2 <= far:
                send(flows(g, s + 2), worked[-1])
    names = flows(0, far)
    worked.append(compute(names, [held[n] for n in names], worked[-1]))

    back = {}

    def give(names, *deps):
        arrived = [back[n[:2]] for n in names if n[:2] in back]
        arrived = tie(arrived, *deps) if arrived else [None] * len(names)
        for (d, h, s), old in zip(names, arrived):
            part = done[d, h, s]
            if old is not None:
                part = (old.astype(jnp.float32) + part).astype(jnp.bfloat16)
            back[d, h] = lax.ppermute(part, "ep", perm[1 - d])

    give(flows(1, far - 1))
    give(flows(0, far))
    for s in range(far - 1, 0, -1):
        if s > 1:
            give(flows(1, s - 1), worked[-1])
        give(flows(0, s), *([back[f] for f in groups[1]] if s == 1 else []))
    compute([(0, 0, 0), (0, 1, 0)], [packed], worked[-1])
    out = [
        (done[0, h, 0] + back[0, h].astype(jnp.float32) + back[1, h].astype(jnp.float32)).astype(jnp.bfloat16)
        for h in range(2)
    ]
    return jnp.concatenate(out, axis=0)


def solution(mesh):
    rows = P(("dp", "ep"), None)
    stacks = P(("dp", "ep"), None, None)
    return jax.shard_map(
        on_device,
        mesh=mesh,
        in_specs=(rows, rows, rows, stacks, stacks, stacks, P()),
        out_specs=rows,
        check_vma=False,
    )
```

```python
import functools

import jax
import jax.numpy as jnp
from jax import lax
from jax.experimental import pallas as pl
from jax.experimental.pallas import tpu as pltpu
from jax.sharding import PartitionSpec as P

LANES = 128
TILE = 16


def pack_kernel(tokens_ref, scores_ref, out_ref):
    rows, width = tokens_ref.shape
    chips = scores_ref.shape[0] // 2
    half = rows // 2
    lane = lax.broadcasted_iota(jnp.int32, (chips, LANES), 1)
    even, odd = (scores_ref[pl.ds(i, chips, stride=2), :] for i in range(2))
    at = 0
    for h in range(2):
        for g in range(0, half, TILE):
            for j in range(0, width, LANES):
                out_ref[pl.ds(at, TILE), :] = tokens_ref[pl.ds(h * half + g, TILE), pl.ds(j, LANES)]
                at += TILE
        first, second = (even, pltpu.roll(odd, half, 1)) if h == 0 else (pltpu.roll(even, half, 1), odd)
        scores = jnp.where(lane < half, first, second)
        high = scores.astype(jnp.bfloat16).astype(jnp.float32)
        tail = jnp.concatenate([high, scores - high], axis=0).astype(jnp.bfloat16)
        out_ref[pl.ds(at, 2 * chips), :] = tail
        at += 2 * chips


def pack(tokens, expert_ids, gate_scores, partner):
    scores = jnp.sum(jnp.where(expert_ids.T[None] == partner[:, None, None], gate_scores.T[None], 0.0), axis=1)
    rows, width = tokens.shape
    near = pl.BlockSpec(memory_space=pltpu.VMEM)
    return pl.pallas_call(
        pack_kernel,
        in_specs=[near, near],
        out_specs=near,
        out_shape=jax.ShapeDtypeStruct((rows * width // LANES + 2 * scores.shape[0], LANES), jnp.bfloat16),
        compiler_params=pltpu.CompilerParams(vmem_limit_bytes=4 * 2**20),
    )(tokens, scores)


def load_kernel(*refs):
    n = len(refs) // 2
    sources, targets, sems = refs[:n], refs[n : 2 * n], refs[-1]
    copies = [pltpu.make_async_copy(a, b, sems.at[i]) for i, (a, b) in enumerate(zip(sources, targets))]
    for copy in copies:
        copy.start()
    for copy in copies:
        copy.wait()


def load(arrays):
    return pl.pallas_call(
        load_kernel,
        in_specs=[pl.BlockSpec(memory_space=pltpu.HBM)] * len(arrays),
        out_specs=[pl.BlockSpec(memory_space=pltpu.VMEM)] * len(arrays),
        out_shape=[jax.ShapeDtypeStruct(a.shape, a.dtype) for a in arrays],
        scratch_shapes=[pltpu.SemaphoreType.DMA((len(arrays),))],
        compiler_params=pltpu.CompilerParams(vmem_limit_bytes=16 * 2**20),
        cost_estimate=pl.CostEstimate(
            flops=0, bytes_accessed=sum(a.size * a.dtype.itemsize for a in arrays), transcendentals=0
        ),
    )(*arrays)


def split_kernel(*refs):
    n = len(refs) // 3
    for i, block_ref in enumerate(refs[:n]):
        size = block_ref.shape[0] // 2
        for h in range(2):
            refs[n + 2 * i + h][...] = block_ref[pl.ds(h * size, size), :]


def split(blocks, flops):
    size, width = blocks[0].shape[0] // 2, blocks[0].shape[1]
    near = pl.BlockSpec(memory_space=pltpu.VMEM)
    return pl.pallas_call(
        split_kernel,
        in_specs=[near] * len(blocks),
        out_specs=[near] * (2 * len(blocks)),
        out_shape=[jax.ShapeDtypeStruct((size, width), jnp.bfloat16)] * (2 * len(blocks)),
        compiler_params=pltpu.CompilerParams(vmem_limit_bytes=6 * 2**20),
        cost_estimate=pl.CostEstimate(flops=flops, bytes_accessed=2**20, transcendentals=0),
    )(*blocks)


def ffn_kernel(n_in, n_out, n_dev, *refs):
    x_refs, weights, refs = refs[:n_in], refs[n_in : n_in + 6], refs[n_in + 6 :]
    out_refs, (rows, total) = refs[:n_out], refs[n_out:]
    half, width = out_refs[0].shape
    me = lax.axis_index("ep")
    chip, core = me // 2, me % 2
    row = lax.broadcasted_iota(jnp.int32, (n_dev, LANES), 0)
    hit = (row == chip) | (row == chip + n_dev // 2)
    columns = []
    for x_ref in x_refs:
        at = 0
        while at < x_ref.shape[0]:
            for g in range(0, half, TILE):
                for j in range(0, width, LANES):
                    rows[pl.ds(len(columns) * half + g, TILE), pl.ds(j, LANES)] = x_ref[pl.ds(at, TILE), :]
                    at += TILE
            tail = jnp.where(hit, x_ref[pl.ds(at, n_dev), :].astype(jnp.float32), 0.0)
            both = jnp.broadcast_to(jnp.sum(tail, axis=0, keepdims=True), (LANES, LANES)).T[:, 0:1]
            columns.append((both[:half], both[half:]))
            at += n_dev
    first, second = (jnp.concatenate([pair[i] for pair in columns], axis=0) for i in range(2))
    for expert in range(2):
        score = jnp.where(core == expert, first, second)
        gate_ref, up_ref, down_ref = weights[3 * expert : 3 * expert + 3]
        x = rows[...]
        gate = jnp.dot(x, gate_ref[0], preferred_element_type=jnp.float32)
        up = jnp.dot(x, up_ref[0], preferred_element_type=jnp.float32)
        hidden = (gate / (1.0 + jnp.exp(-gate)) * up).astype(jnp.bfloat16)
        out = jnp.dot(hidden, down_ref[0], preferred_element_type=jnp.float32) * score
        if expert == 0:
            total[...] = out
        else:
            out = total[...] + out
            for i, out_ref in enumerate(out_refs):
                out_ref[...] = out[i * half : (i + 1) * half].astype(out_ref.dtype)


def ffn(blocks, half, kinds, own, other, n_dev):
    _, width, ff = own[0].shape
    n_in, n_out = len(blocks), len(kinds)
    m = n_out * half
    near = pl.BlockSpec(memory_space=pltpu.VMEM)
    return pl.pallas_call(
        functools.partial(ffn_kernel, n_in, n_out, n_dev),
        in_specs=[near] * (n_in + 6),
        out_specs=[near] * n_out,
        out_shape=[jax.ShapeDtypeStruct((half, width), kind) for kind in kinds],
        scratch_shapes=[pltpu.VMEM((m, width), jnp.bfloat16), pltpu.VMEM((m, width), jnp.float32)],
        compiler_params=pltpu.CompilerParams(vmem_limit_bytes=16 * 2**20),
        cost_estimate=pl.CostEstimate(
            flops=12 * m * width * ff, bytes_accessed=12 * width * ff + 6 * m * width, transcendentals=2 * m * ff
        ),
    )(*blocks, *own, *other)


def ring_order(chips):
    return list(range(0, chips, 2)) + list(range(1, chips, 2))[::-1]


def on_device(tokens, expert_ids, gate_scores, gate_weight, up_weight, down_weight, partner):
    n_dev = lax.axis_size("ep")
    chips = n_dev // 2
    far = chips // 2
    order = ring_order(chips)

    def shift(by):
        return [(order[i] * 2 + k, order[(i + by) % chips] * 2 + k) for i in range(chips) for k in range(2)]

    perm = (shift(1), shift(-1))
    swap = [(i, i ^ 1) for i in range(n_dev)]
    own = (gate_weight, up_weight, down_weight)

    def tie(value, *deps):
        return lax.optimization_barrier((value, deps))[0]

    half = tokens.shape[0] // 2
    other = [lax.ppermute(w, "ep", swap) for w in own]
    packed = pack(tokens, expert_ids, gate_scores, partner)
    first = [lax.ppermute(packed, "ep", perm[d]) for d in range(2)]
    own = load(own)
    held = dict(zip([(d, h, 1) for d in range(2) for h in range(2)], split(first, 3 * 10**10)))
    last = {(d, h): far if d == h else far - 1 for d in range(2) for h in range(2)}
    done = {}

    def compute(names, blocks, *deps):
        kinds = [jnp.bfloat16 if n[2] and n[2] == last[n[:2]] else jnp.float32 for n in names]
        blocks = tie(blocks, *deps) if deps else blocks
        done.update(zip(names, ffn(blocks, half, kinds, own, other, n_dev)))
        return done[names[0]]

    def send(names, *deps):
        for d, h, s in names:
            held[d, h, s] = lax.ppermute(tie(held[d, h, s - 1], *deps), "ep", perm[d])

    groups = ([(0, 0), (1, 1)], [(1, 0), (0, 1)])

    def flows(g, s):
        return [(d, h, s) for d, h in groups[g] if s <= last[d, h]]

    for g in range(2):
        send(flows(g, 2), *(other if g else other[:2]), *own)
    worked = []
    for s in range(1, far):
        for g in range(2):
            names = flows(g, s)
            worked.append(compute(names, [held[n] for n in names], *worked[-1:]))
            if s + 2 <= far:
                send(flows(g, s + 2), worked[-1])
    names = flows(0, far)
    worked.append(compute(names, [held[n] for n in names], worked[-1]))

    back = {}

    def give(names, *deps):
        arrived = [back[n[:2]] for n in names if n[:2] in back]
        arrived = tie(arrived, *deps) if arrived else [None] * len(names)
        for (d, h, s), old in zip(names, arrived):
            part = done[d, h, s]
            if old is not None:
                part = (old.astype(jnp.float32) + part).astype(jnp.bfloat16)
            back[d, h] = lax.ppermute(part, "ep", perm[1 - d])

    give(flows(1, far - 1))
    give(flows(0, far))
    for s in range(far - 1, 0, -1):
        if s > 1:
            give(flows(1, s - 1), worked[-1])
        give(flows(0, s), *([back[f] for f in groups[1]] if s == 1 else []))
    compute([(0, 0, 0), (0, 1, 0)], [packed], worked[-1])
    out = [
        (done[0, h, 0] + back[0, h].astype(jnp.float32) + back[1, h].astype(jnp.float32)).astype(jnp.bfloat16)
        for h in range(2)
    ]
    return jnp.concatenate(out, axis=0)


def solution(mesh):
    rows = P(("dp", "ep"), None)
    stacks = P(("dp", "ep"), None, None)
    return jax.shard_map(
        on_device,
        mesh=mesh,
        in_specs=(rows, rows, rows, stacks, stacks, stacks, P()),
        out_specs=rows,
        check_vma=False,
    )
```

```python
import functools

import jax
import jax.numpy as jnp
from jax import lax
from jax.experimental import pallas as pl
from jax.experimental.pallas import tpu as pltpu
from jax.sharding import PartitionSpec as P

LANES = 128
TILE = 16


def tail_kernel(scores_ref, out_ref):
    chips, rows = scores_ref.shape[0] // 2, scores_ref.shape[1]
    half = rows // 2
    lane = lax.broadcasted_iota(jnp.int32, (chips, LANES), 1)
    even, odd = (scores_ref[pl.ds(i, chips, stride=2), :] for i in range(2))
    for h in range(2):
        first, second = (even, pltpu.roll(odd, half, 1)) if h == 0 else (pltpu.roll(even, half, 1), odd)
        scores = jnp.where(lane < half, first, second)
        high = scores.astype(jnp.bfloat16).astype(jnp.float32)
        tail = jnp.concatenate([high, scores - high], axis=0).astype(jnp.bfloat16)
        out_ref[pl.ds(h * 2 * chips, 2 * chips), :] = tail


def tail_of(expert_ids, gate_scores, partner):
    scores = jnp.sum(jnp.where(expert_ids.T[None] == partner[:, None, None], gate_scores.T[None], 0.0), axis=1)
    near = pl.BlockSpec(memory_space=pltpu.VMEM)
    return pl.pallas_call(
        tail_kernel,
        in_specs=[near],
        out_specs=near,
        out_shape=jax.ShapeDtypeStruct((2 * scores.shape[0], LANES), jnp.bfloat16),
        compiler_params=pltpu.CompilerParams(vmem_limit_bytes=2 * 2**20),
    )(scores)


def pack_kernel(n, *refs):
    block_refs, tail_refs, out_refs = refs[:n], refs[n : 2 * n], refs[2 * n :]
    for i, (block_ref, tail_ref) in enumerate(zip(block_refs, tail_refs)):
        half, extra = block_ref.shape[0] // 2, tail_ref.shape[0] // 2
        for h in range(2):
            out_ref = out_refs[2 * i + h]
            at = 0
            for g in range(0, half, TILE):
                for j in range(0, block_ref.shape[1], LANES):
                    out_ref[pl.ds(at, TILE), :] = block_ref[pl.ds(h * half + g, TILE), pl.ds(j, LANES)]
                    at += TILE
            out_ref[pl.ds(at, extra), :] = tail_ref[pl.ds(h * extra, extra), :]


def pack(blocks, tails, flops):
    rows, width = blocks[0].shape
    near = pl.BlockSpec(memory_space=pltpu.VMEM)
    size = rows // 2 * width // LANES + tails[0].shape[0] // 2
    return pl.pallas_call(
        functools.partial(pack_kernel, len(blocks)),
        in_specs=[near] * (2 * len(blocks)),
        out_specs=[near] * (2 * len(blocks)),
        out_shape=[jax.ShapeDtypeStruct((size, LANES), jnp.bfloat16)] * (2 * len(blocks)),
        compiler_params=pltpu.CompilerParams(vmem_limit_bytes=6 * 2**20),
        cost_estimate=pl.CostEstimate(flops=flops, bytes_accessed=2**20, transcendentals=0),
    )(*blocks, *tails)


def load_kernel(*refs):
    n = len(refs) // 2
    sources, targets, sems = refs[:n], refs[n : 2 * n], refs[-1]
    copies = [pltpu.make_async_copy(a, b, sems.at[i]) for i, (a, b) in enumerate(zip(sources, targets))]
    for copy in copies:
        copy.start()
    for copy in copies:
        copy.wait()


def load(arrays):
    return pl.pallas_call(
        load_kernel,
        in_specs=[pl.BlockSpec(memory_space=pltpu.HBM)] * len(arrays),
        out_specs=[pl.BlockSpec(memory_space=pltpu.VMEM)] * len(arrays),
        out_shape=[jax.ShapeDtypeStruct(a.shape, a.dtype) for a in arrays],
        scratch_shapes=[pltpu.SemaphoreType.DMA((len(arrays),))],
        compiler_params=pltpu.CompilerParams(vmem_limit_bytes=16 * 2**20),
        cost_estimate=pl.CostEstimate(
            flops=0, bytes_accessed=sum(a.size * a.dtype.itemsize for a in arrays), transcendentals=0
        ),
    )(*arrays)


def ffn_kernel(n_in, n_out, n_dev, *refs):
    x_refs, weights, refs = refs[:n_in], refs[n_in : n_in + 6], refs[n_in + 6 :]
    out_refs, (rows, total) = refs[:n_out], refs[n_out:]
    half, width = out_refs[0].shape
    me = lax.axis_index("ep")
    chip, core = me // 2, me % 2
    row = lax.broadcasted_iota(jnp.int32, (n_dev, LANES), 0)
    hit = (row == chip) | (row == chip + n_dev // 2)
    columns = []
    for x_ref in x_refs:
        at = 0
        while at < x_ref.shape[0]:
            for g in range(0, half, TILE):
                for j in range(0, width, LANES):
                    rows[pl.ds(len(columns) * half + g, TILE), pl.ds(j, LANES)] = x_ref[pl.ds(at, TILE), :]
                    at += TILE
            tail = jnp.where(hit, x_ref[pl.ds(at, n_dev), :].astype(jnp.float32), 0.0)
            both = jnp.broadcast_to(jnp.sum(tail, axis=0, keepdims=True), (LANES, LANES)).T[:, 0:1]
            columns.append((both[:half], both[half:]))
            at += n_dev
    first, second = (jnp.concatenate([pair[i] for pair in columns], axis=0) for i in range(2))
    for expert in range(2):
        score = jnp.where(core == expert, first, second)
        gate_ref, up_ref, down_ref = weights[3 * expert : 3 * expert + 3]
        x = rows[...]
        gate = jnp.dot(x, gate_ref[0], preferred_element_type=jnp.float32)
        up = jnp.dot(x, up_ref[0], preferred_element_type=jnp.float32)
        hidden = (gate / (1.0 + jnp.exp(-gate)) * up).astype(jnp.bfloat16)
        out = jnp.dot(hidden, down_ref[0], preferred_element_type=jnp.float32) * score
        if expert == 0:
            total[...] = out
        else:
            out = total[...] + out
            for i, out_ref in enumerate(out_refs):
                out_ref[...] = out[i * half : (i + 1) * half].astype(out_ref.dtype)


def ffn(blocks, half, kinds, own, other, n_dev):
    _, width, ff = own[0].shape
    n_in, n_out = len(blocks), len(kinds)
    m = n_out * half
    near = pl.BlockSpec(memory_space=pltpu.VMEM)
    return pl.pallas_call(
        functools.partial(ffn_kernel, n_in, n_out, n_dev),
        in_specs=[near] * (n_in + 6),
        out_specs=[near] * n_out,
        out_shape=[jax.ShapeDtypeStruct((half, width), kind) for kind in kinds],
        scratch_shapes=[pltpu.VMEM((m, width), jnp.bfloat16), pltpu.VMEM((m, width), jnp.float32)],
        compiler_params=pltpu.CompilerParams(vmem_limit_bytes=16 * 2**20),
        cost_estimate=pl.CostEstimate(
            flops=12 * m * width * ff, bytes_accessed=12 * width * ff + 6 * m * width, transcendentals=2 * m * ff
        ),
    )(*blocks, *own, *other)


def ring_order(chips):
    return list(range(0, chips, 2)) + list(range(1, chips, 2))[::-1]


def on_device(tokens, expert_ids, gate_scores, gate_weight, up_weight, down_weight, partner):
    n_dev = lax.axis_size("ep")
    chips = n_dev // 2
    far = chips // 2
    order = ring_order(chips)

    def shift(by):
        return [(order[i] * 2 + k, order[(i + by) % chips] * 2 + k) for i in range(chips) for k in range(2)]

    perm = (shift(1), shift(-1))
    swap = [(i, i ^ 1) for i in range(n_dev)]
    own = (gate_weight, up_weight, down_weight)

    def tie(value, *deps):
        return lax.optimization_barrier((value, deps))[0]

    half = tokens.shape[0] // 2
    first = [lax.ppermute(tokens, "ep", perm[d]) for d in range(2)]
    tail = tail_of(expert_ids, gate_scores, partner)
    tails = [lax.ppermute(tail, "ep", perm[d]) for d in range(2)]
    other = [lax.ppermute(w if i == 0 else tie(w, *tails), "ep", swap) for i, w in enumerate(own)]
    own = load(own)
    held = dict(zip([(d, h, 1) for d in range(2) for h in range(2)], pack(first, tails, 5 * 10**10)))
    last = {(d, h): far if d == h else far - 1 for d in range(2) for h in range(2)}
    done = {}

    def compute(names, blocks, *deps):
        kinds = [jnp.bfloat16 if n[2] and n[2] == last[n[:2]] else jnp.float32 for n in names]
        blocks = tie(blocks, *deps) if deps else blocks
        done.update(zip(names, ffn(blocks, half, kinds, own, other, n_dev)))
        return done[names[0]]

    def send(names, *deps):
        for d, h, s in names:
            held[d, h, s] = lax.ppermute(tie(held[d, h, s - 1], *deps), "ep", perm[d])

    groups = ([(0, 0), (1, 1)], [(1, 0), (0, 1)])

    def flows(g, s):
        return [(d, h, s) for d, h in groups[g] if s <= last[d, h]]

    for g in range(2):
        send(flows(g, 2), *([other[0], *own] if g == 0 else other[:2]))
    worked = []
    for s in range(1, far):
        for g in range(2):
            names = flows(g, s)
            if s > 1:
                worked.append(compute(names, [held[n] for n in names], *worked[-1:]))
            if s + 2 <= far:
                send(flows(g, s + 2), *worked[-1:])
    names = flows(0, far)
    worked.append(compute(names, [held[n] for n in names], worked[-1]))
    for g in (1, 0):
        names = flows(g, 1)
        worked.append(compute(names, [held[n] for n in names], worked[-1]))
    k_far = worked[-3]

    back = {}

    def give(names, *deps):
        arrived = [back[n[:2]] for n in names if n[:2] in back]
        arrived = tie(arrived, *deps) if arrived else [None] * len(names)
        for (d, h, s), old in zip(names, arrived):
            part = done[d, h, s]
            if old is not None:
                part = (old.astype(jnp.float32) + part).astype(jnp.bfloat16)
            back[d, h] = lax.ppermute(part, "ep", perm[1 - d])

    give(flows(1, far - 1))
    give(flows(0, far))
    for s in range(far - 1, 0, -1):
        if s > 1:
            give(flows(1, s - 1), k_far)
        give(flows(0, s), *([back[f] for f in groups[1]] if s == 1 else []))
    compute([(0, 0, 0), (0, 1, 0)], pack([tokens], [tail], 0), worked[-1])
    out = [
        (done[0, h, 0] + back[0, h].astype(jnp.float32) + back[1, h].astype(jnp.float32)).astype(jnp.bfloat16)
        for h in range(2)
    ]
    return jnp.concatenate(out, axis=0)


def solution(mesh):
    rows = P(("dp", "ep"), None)
    stacks = P(("dp", "ep"), None, None)
    return jax.shard_map(
        on_device,
        mesh=mesh,
        in_specs=(rows, rows, rows, stacks, stacks, stacks, P()),
        out_specs=rows,
        check_vma=False,
    )
```

```python
import functools

import jax
import jax.numpy as jnp
from jax import lax
from jax.experimental import pallas as pl
from jax.experimental.pallas import tpu as pltpu
from jax.sharding import PartitionSpec as P

LANES = 128
TILE = 16


def tail_kernel(scores_ref, out_ref):
    chips, rows = scores_ref.shape[0] // 2, scores_ref.shape[1]
    half = rows // 2
    lane = lax.broadcasted_iota(jnp.int32, (chips, LANES), 1)
    even, odd = (scores_ref[pl.ds(i, chips, stride=2), :] for i in range(2))
    for h in range(2):
        first, second = (even, pltpu.roll(odd, half, 1)) if h == 0 else (pltpu.roll(even, half, 1), odd)
        scores = jnp.where(lane < half, first, second)
        high = scores.astype(jnp.bfloat16).astype(jnp.float32)
        tail = jnp.concatenate([high, scores - high], axis=0).astype(jnp.bfloat16)
        out_ref[pl.ds(h * 2 * chips, 2 * chips), :] = tail


def tail_of(expert_ids, gate_scores, partner):
    scores = jnp.sum(jnp.where(expert_ids.T[None] == partner[:, None, None], gate_scores.T[None], 0.0), axis=1)
    near = pl.BlockSpec(memory_space=pltpu.VMEM)
    return pl.pallas_call(
        tail_kernel,
        in_specs=[near],
        out_specs=near,
        out_shape=jax.ShapeDtypeStruct((2 * scores.shape[0], LANES), jnp.bfloat16),
        compiler_params=pltpu.CompilerParams(vmem_limit_bytes=2 * 2**20),
    )(scores)


def pack_kernel(n, *refs):
    block_refs, tail_refs, out_refs = refs[:n], refs[n : 2 * n], refs[2 * n :]
    for i, (block_ref, tail_ref) in enumerate(zip(block_refs, tail_refs)):
        half, extra = block_ref.shape[0] // 2, tail_ref.shape[0] // 2
        for h in range(2):
            out_ref = out_refs[2 * i + h]
            at = 0
            for g in range(0, half, TILE):
                for j in range(0, block_ref.shape[1], LANES):
                    out_ref[pl.ds(at, TILE), :] = block_ref[pl.ds(h * half + g, TILE), pl.ds(j, LANES)]
                    at += TILE
            out_ref[pl.ds(at, extra), :] = tail_ref[pl.ds(h * extra, extra), :]


def pack(blocks, tails, flops):
    rows, width = blocks[0].shape
    near = pl.BlockSpec(memory_space=pltpu.VMEM)
    size = rows // 2 * width // LANES + tails[0].shape[0] // 2
    return pl.pallas_call(
        functools.partial(pack_kernel, len(blocks)),
        in_specs=[near] * (2 * len(blocks)),
        out_specs=[near] * (2 * len(blocks)),
        out_shape=[jax.ShapeDtypeStruct((size, LANES), jnp.bfloat16)] * (2 * len(blocks)),
        compiler_params=pltpu.CompilerParams(vmem_limit_bytes=6 * 2**20),
        cost_estimate=pl.CostEstimate(flops=flops, bytes_accessed=2**20, transcendentals=0),
    )(*blocks, *tails)


def load_kernel(*refs):
    n = len(refs) // 2
    sources, targets, sems = refs[:n], refs[n : 2 * n], refs[-1]
    copies = [pltpu.make_async_copy(a, b, sems.at[i]) for i, (a, b) in enumerate(zip(sources, targets))]
    for copy in copies:
        copy.start()
    for copy in copies:
        copy.wait()


def load(arrays):
    return pl.pallas_call(
        load_kernel,
        in_specs=[pl.BlockSpec(memory_space=pltpu.HBM)] * len(arrays),
        out_specs=[pl.BlockSpec(memory_space=pltpu.VMEM)] * len(arrays),
        out_shape=[jax.ShapeDtypeStruct(a.shape, a.dtype) for a in arrays],
        scratch_shapes=[pltpu.SemaphoreType.DMA((len(arrays),))],
        compiler_params=pltpu.CompilerParams(vmem_limit_bytes=16 * 2**20),
        cost_estimate=pl.CostEstimate(
            flops=0, bytes_accessed=sum(a.size * a.dtype.itemsize for a in arrays), transcendentals=0
        ),
    )(*arrays)


def ffn_kernel(n_in, n_out, n_dev, *refs):
    x_refs, weights, refs = refs[:n_in], refs[n_in : n_in + 6], refs[n_in + 6 :]
    out_refs, (rows, total) = refs[:n_out], refs[n_out:]
    half, width = out_refs[0].shape
    me = lax.axis_index("ep")
    chip, core = me // 2, me % 2
    row = lax.broadcasted_iota(jnp.int32, (n_dev, LANES), 0)
    hit = (row == chip) | (row == chip + n_dev // 2)
    columns = []
    for x_ref in x_refs:
        at = 0
        while at < x_ref.shape[0]:
            for g in range(0, half, TILE):
                for j in range(0, width, LANES):
                    rows[pl.ds(len(columns) * half + g, TILE), pl.ds(j, LANES)] = x_ref[pl.ds(at, TILE), :]
                    at += TILE
            tail = jnp.where(hit, x_ref[pl.ds(at, n_dev), :].astype(jnp.float32), 0.0)
            both = jnp.broadcast_to(jnp.sum(tail, axis=0, keepdims=True), (LANES, LANES)).T[:, 0:1]
            columns.append((both[:half], both[half:]))
            at += n_dev
    first, second = (jnp.concatenate([pair[i] for pair in columns], axis=0) for i in range(2))
    for expert in range(2):
        score = jnp.where(core == expert, first, second)
        gate_ref, up_ref, down_ref = weights[3 * expert : 3 * expert + 3]
        x = rows[...]
        gate = jnp.dot(x, gate_ref[0], preferred_element_type=jnp.float32)
        up = jnp.dot(x, up_ref[0], preferred_element_type=jnp.float32)
        hidden = (gate / (1.0 + jnp.exp(-gate)) * up).astype(jnp.bfloat16)
        out = jnp.dot(hidden, down_ref[0], preferred_element_type=jnp.float32) * score
        if expert == 0:
            total[...] = out
        else:
            out = total[...] + out
            for i, out_ref in enumerate(out_refs):
                out_ref[...] = out[i * half : (i + 1) * half].astype(out_ref.dtype)


def ffn(blocks, half, kinds, own, other, n_dev):
    _, width, ff = own[0].shape
    n_in, n_out = len(blocks), len(kinds)
    m = n_out * half
    near = pl.BlockSpec(memory_space=pltpu.VMEM)
    return pl.pallas_call(
        functools.partial(ffn_kernel, n_in, n_out, n_dev),
        in_specs=[near] * (n_in + 6),
        out_specs=[near] * n_out,
        out_shape=[jax.ShapeDtypeStruct((half, width), kind) for kind in kinds],
        scratch_shapes=[pltpu.VMEM((m, width), jnp.bfloat16), pltpu.VMEM((m, width), jnp.float32)],
        compiler_params=pltpu.CompilerParams(vmem_limit_bytes=16 * 2**20),
        cost_estimate=pl.CostEstimate(
            flops=12 * m * width * ff, bytes_accessed=12 * width * ff + 6 * m * width, transcendentals=2 * m * ff
        ),
    )(*blocks, *own, *other)


def finish_kernel(own_ref, ahead_ref, behind_ref, *refs):
    total = own_ref[...] + ahead_ref[...].astype(jnp.float32) + behind_ref[...].astype(jnp.float32)
    refs[-1][...] = total.astype(refs[-1].dtype)


def finish(h, out, own, ahead, behind):
    half, width = own.shape
    near = pl.BlockSpec(memory_space=pltpu.VMEM)
    return pl.pallas_call(
        finish_kernel,
        grid=(1,),
        in_specs=[near] * 3 + ([] if out is None else [pl.BlockSpec(memory_space=pl.ANY)]),
        out_specs=pl.BlockSpec((half, width), lambda i: (h, 0)),
        out_shape=jax.ShapeDtypeStruct((2 * half, width), jnp.bfloat16),
        input_output_aliases={} if out is None else {3: 0},
        compiler_params=pltpu.CompilerParams(vmem_limit_bytes=6 * 2**20),
    )(own, ahead, behind, *([] if out is None else [out]))


def ring_order(chips):
    return list(range(0, chips, 2)) + list(range(1, chips, 2))[::-1]


def on_device(tokens, expert_ids, gate_scores, gate_weight, up_weight, down_weight, partner):
    n_dev = lax.axis_size("ep")
    chips = n_dev // 2
    far = chips // 2
    order = ring_order(chips)

    def shift(by):
        return [(order[i] * 2 + k, order[(i + by) % chips] * 2 + k) for i in range(chips) for k in range(2)]

    perm = (shift(1), shift(-1))
    swap = [(i, i ^ 1) for i in range(n_dev)]
    own = (gate_weight, up_weight, down_weight)

    def tie(value, *deps):
        return lax.optimization_barrier((value, deps))[0]

    half = tokens.shape[0] // 2
    first = [lax.ppermute(tokens, "ep", perm[d]) for d in range(2)]
    tail = tail_of(expert_ids, gate_scores, partner)
    tails = [lax.ppermute(tail, "ep", perm[d]) for d in range(2)]
    other = [lax.ppermute(w if i == 0 else tie(w, *tails), "ep", swap) for i, w in enumerate(own)]
    own = load(own)
    held = dict(zip([(d, h, 1) for d in range(2) for h in range(2)], pack(first, tails, 5 * 10**10)))
    last = {(d, h): far if d == h else far - 1 for d in range(2) for h in range(2)}
    done = {}

    def compute(names, blocks, *deps):
        kinds = [jnp.bfloat16 if n[2] and n[2] == last[n[:2]] else jnp.float32 for n in names]
        blocks = tie(blocks, *deps) if deps else blocks
        done.update(zip(names, ffn(blocks, half, kinds, own, other, n_dev)))
        return done[names[0]]

    def send(names, *deps):
        for d, h, s in names:
            held[d, h, s] = lax.ppermute(tie(held[d, h, s - 1], *deps), "ep", perm[d])

    groups = ([(0, 0), (1, 1)], [(1, 0), (0, 1)])

    def flows(g, s):
        return [(d, h, s) for d, h in groups[g] if s <= last[d, h]]

    for g in range(2):
        send(flows(g, 2), *([other[0], *own] if g == 0 else other[:2]))
    worked = []
    for s in range(1, far):
        for g in range(2):
            names = flows(g, s)
            if s > 1:
                worked.append(compute(names, [held[n] for n in names], *worked[-1:]))
            if s + 2 <= far:
                send(flows(g, s + 2), *worked[-1:])
    names = flows(0, far)
    worked.append(compute(names, [held[n] for n in names], worked[-1]))
    for g in (1, 0):
        names = flows(g, 1)
        worked.append(compute(names, [held[n] for n in names], worked[-1]))
    k_far = worked[-3]

    back = {}

    def give(names, *deps):
        arrived = [back[n[:2]] for n in names if n[:2] in back]
        arrived = tie(arrived, *deps) if arrived else [None] * len(names)
        for (d, h, s), old in zip(names, arrived):
            part = done[d, h, s]
            if old is not None:
                part = (old.astype(jnp.float32) + part).astype(jnp.bfloat16)
            back[d, h] = lax.ppermute(part, "ep", perm[1 - d])

    give(flows(1, far - 1))
    give(flows(0, far))
    for s in range(far - 1, 0, -1):
        if s > 1:
            give(flows(1, s - 1), k_far)
        give(flows(0, s), *([back[f] for f in groups[1]] if s == 1 else []))
    compute([(0, 0, 0), (0, 1, 0)], pack([tokens], [tail], 0), worked[-1])
    out = None
    for h in range(2):
        out = finish(h, out, done[0, h, 0], back[0, h], back[1, h])
    return out


def solution(mesh):
    rows = P(("dp", "ep"), None)
    stacks = P(("dp", "ep"), None, None)
    return jax.shard_map(
        on_device,
        mesh=mesh,
        in_specs=(rows, rows, rows, stacks, stacks, stacks, P()),
        out_specs=rows,
        check_vma=False,
    )
```
